32 devices in a mesh: section: 2 (over y), ctx: 4 (over z), tp: 4 (over x, core).
Axes of the slice: x: 2, y: 2, z: 4, core: 2. Of those that a mesh axis runs over, the one named last changes fastest.
Arguments:
- section_input: bfloat16 [4, 4096, 768], P(None, 'ctx'), may hold values from -6 to 6
- cotangent: bfloat16 [4, 4096, 768], P(None, 'ctx'), may hold values from -6 to 6
- counts: int32 [4, 4], replicated, may hold values from 256 to 1024, as said below
- norm_gain: bfloat16 [2, 2, 768], P('section', None, 'ctx'), may hold values from 0.5 to 1.5
- vector_bias: bfloat16 [2, 4, 768], P('section', None, 'ctx'), may hold values from -4 to 4
- qkv_weight: bfloat16 [2, 3, 768, 768], P('section', None, 'ctx', 'tp'), may hold values from -0.21875 to 0.21875
- head_bias: bfloat16 [2, 2, 12, 64], P('section', None, 'tp', 'ctx'), may hold values from -0.3125 to 0.3125
- out_weight: bfloat16 [2, 768, 768], P('section', 'tp', 'ctx'), may hold values from -6 to 6
- up_weight: bfloat16 [2, 768, 3072], P('section', 'ctx', 'tp'), may hold values from -0.21875 to 0.21875
- up_bias: bfloat16 [2, 48, 64], P('section', 'tp', 'ctx'), may hold values from -4 to 4
- down_weight: bfloat16 [2, 3072, 768], P('section', 'tp', 'ctx'), may hold values from -0.109375 to 0.109375
Outputs:
- acts: bfloat16 [2, 4, 4096, 768], P('section', None, 'ctx')
- in_grads: bfloat16 [2, 4, 4096, 768], P('section', None, 'ctx')
- grad_norm_gain: float32 [2, 2, 768], P('section', None, 'ctx')
- grad_vector_bias: float32 [2, 4, 768], P('section', None, 'ctx')
- grad_qkv: float32 [2, 3, 768, 768], P('section', None, 'ctx', 'tp')
- grad_head_bias: float32 [2, 2, 12, 64], P('section', None, 'tp', 'ctx')
- grad_out: float32 [2, 768, 768], P('section', 'tp', 'ctx')
- grad_up: float32 [2, 768, 3072], P('section', 'ctx', 'tp')
- grad_up_bias: float32 [2, 48, 64], P('section', 'tp', 'ctx')
- grad_down: float32 [2, 3072, 768], P('section', 'tp', 'ctx')
The draws below stay inside these ranges and needn't reach their ends.
Inputs may be any that keep to these rules, and one draw needn't show every extreme that they name: counts[m, i] is the number of live rows of device i of ctx in micro-batch m: its first counts[m, i] row slots hold tokens, the others are padding. Each row of counts sums to 2048, and its largest entry is 1024.
All inputs are finite; a program needn't handle non-finite values.
Results may differ from the reference program's by a relative error of at most 0.025.
Values may be sent and summed in bfloat16 or wider, within the bound.
A program may use at most 320 MiB of HBM per device.

```python
import math
import jax
import jax.numpy as jnp
from jax import lax

D = 768
H = 12
HD = 64
FF = 3072
MB = 4
SEQ = 2048
TOK_SHARE = 512
CAP = 1024
ROWS = 4096
N_SECTION = 2
N_CTX = 4


def draw_counts(key, part):
    key = jax.random.fold_in(key, 7)
    table_rows = []
    for micro_index in range(MB):
        first_key, second_key = jax.random.split(jax.random.fold_in(key, micro_index))
        fixed_part = jnp.array([2 * TOK_SHARE, TOK_SHARE // 2, TOK_SHARE - TOK_SHARE // 2, TOK_SHARE], jnp.int32)
        pair_count = (N_CTX - 4) // 2
        spread = jax.random.randint(first_key, (pair_count,), 0, TOK_SHARE // 2 + 1)
        paired = jnp.stack([TOK_SHARE + spread, TOK_SHARE - spread], axis=1).reshape(-1).astype(jnp.int32)
        ordering = jax.random.permutation(second_key, N_CTX)
        table_rows.append(jnp.concatenate([fixed_part, paired])[ordering])
    return jnp.stack(table_rows).astype(jnp.int32)


def block_levels(rng, dims, cuts, least, largest):
    level, own = 1.0, jax.random.fold_in(rng, 6)
    for dim, blocks in cuts:
        draws = jnp.exp(jax.random.uniform(jax.random.fold_in(own, dim), (blocks,), jnp.float32, least / len(cuts), largest / len(cuts)))
        level = level * jnp.repeat(draws, dims[dim] // blocks).reshape([-1 if axis == dim else 1 for axis in range(len(dims))])
    return level


def scatter_about(stream_key, extent, width, most, cuts=(), kind=jnp.bfloat16):
    result = jax.random.normal(stream_key, extent, jnp.float32) * width
    if len(cuts) > 0:
        result = block_levels(stream_key, extent, cuts, -0.22, 0.18) * result
    return jnp.clip(result, min=-most, max=most).astype(kind)


def setup_inputs(seed: int = 0) -> dict:
    splits = jax.random.split(jax.random.key(seed), 12)
    return {
        "section_input": scatter_about(splits[0], (MB, ROWS, D), 1.0, 6.0, ((1, 4),)),
        "cotangent": scatter_about(splits[1], (MB, ROWS, D), 1.0, 6.0, ((1, 4),)),
        "counts": draw_counts(jax.random.fold_in(splits[11], 71), 0),
        "norm_gain": jnp.clip(1.0 + 0.1 * jax.random.normal(splits[3], (N_SECTION, 2, D), jnp.float32), 0.5, 1.5).astype(jnp.bfloat16),
        "vector_bias": scatter_about(splits[4], (N_SECTION, 4, D), 0.3, 4.0, ((0, 2), (2, 4))),
        "qkv_weight": scatter_about(splits[5], (N_SECTION, 3, D, D), D ** -0.5, 0.21875, ((0, 2), (2, 4), (3, 4))),
        "head_bias": scatter_about(splits[6], (N_SECTION, 2, H, HD), (SEQ ** -0.5), 0.3125, ((0, 2), (2, 4), (3, 4))),
        "out_weight": scatter_about(splits[7], (N_SECTION, D, D), (max(1, 3 * D // SEQ)) ** -0.5, 6.0, ((0, 2), (1, 4), (2, 4))),
        "up_weight": scatter_about(splits[8], (N_SECTION, D, FF), D ** -0.5, 0.21875, ((0, 2), (1, 4), (2, 4))),
        "up_bias": scatter_about(splits[9], (N_SECTION, FF // HD, HD), 0.3, 4.0, ((0, 2), (1, 4), (2, 4))),
        "down_weight": scatter_about(splits[10], (N_SECTION, FF, D), FF ** -0.5, 0.109375, ((0, 2), (1, 4), (2, 4))),
    }


PRECISE = lax.Precision.HIGHEST
EPSILON = 1e-06
NEGATIVE_FILL = -1e+30

@jax.custom_vjp
def low(v):
    return lax.optimization_barrier(v.astype(jnp.bfloat16)).astype(jnp.float32)

@jax.custom_vjp
def low_back(v):
    return v

def low_keep(v):
    return (low(v), None)

def low_pass(kept, grad):
    return (grad,)

def back_keep(v):
    return (v, None)

def back_low(kept, grad):
    return (low(grad),)
low.defvjp(low_keep, low_pass)
low_back.defvjp(back_keep, back_low)

def matmul(left, right):
    return jnp.dot(left, right, precision=PRECISE, preferred_element_type=jnp.float32)

def normalize(values, gains, shift):
    center = values - lax.optimization_barrier(jnp.mean(values, axis=-1, keepdims=True))
    spread = lax.optimization_barrier(jnp.mean(center * center, axis=-1, keepdims=True))
    return center * lax.rsqrt(spread + EPSILON) * gains + shift

def attention(queries, key_rows, value_rows, key_live):
    total_rows = queries.shape[0]
    block_size = math.gcd(total_rows, 512)

    def one_block(query_block):
        scores = jnp.einsum('qhd,khd->hqk', query_block, key_rows, precision=PRECISE) * HD ** (-0.5)
        scores = jnp.where(key_live[None, None, :], low_back(scores), NEGATIVE_FILL)
        shifted = jnp.exp(scores - lax.optimization_barrier(jnp.max(scores, axis=-1, keepdims=True)))
        weights = low(shifted / lax.optimization_barrier(jnp.sum(shifted, axis=-1, keepdims=True)))
        return jnp.einsum('hqk,khd->qhd', weights, value_rows, precision=PRECISE)
    blocks = queries.reshape(total_rows // block_size, block_size, H, HD)
    return lax.map(jax.checkpoint(one_block), blocks).reshape(total_rows, H * HD)

def layer_apply(params, residual, live_rows, key_live):
    gains, shifts, qkv_weight, head_bias, out_weight, up_weight, up_bias, down_weight = params
    total_rows = residual.shape[0]
    normed = low(normalize(residual, gains[0], shifts[0]))
    queries = low_back(low(matmul(normed, qkv_weight[0]) + head_bias[0].reshape(-1)))
    key_rows = low_back(low(matmul(normed, qkv_weight[1])))
    value_rows = low_back(low(matmul(normed, qkv_weight[2]) + head_bias[1].reshape(-1)))
    attended = attention(queries.reshape(total_rows, H, HD), key_rows.reshape(total_rows, H, HD), value_rows.reshape(total_rows, H, HD), key_live)
    attended = low_back(low(attended))
    middle = residual + low_back(matmul(attended, out_weight) + shifts[1])
    normed_two = low(normalize(middle, gains[1], shifts[2]))
    expanded = low_back(matmul(normed_two, up_weight) + up_bias.reshape(-1))
    activated = low(jax.nn.gelu(expanded, approximate=False))
    return (middle + low_back(matmul(activated, down_weight) + shifts[3])) * live_rows[:, None]

def reference(section_input, cotangent, counts, norm_gain, vector_bias, qkv_weight, head_bias, out_weight, up_weight, up_bias, down_weight):
    weights = tuple((tensor.astype(jnp.float32) for tensor in (norm_gain, vector_bias, qkv_weight, head_bias, out_weight, up_weight, up_bias, down_weight)))
    section_params = [tuple((tensor[section_number] for tensor in weights)) for section_number in range(2)]
    slot_index = jnp.arange(ROWS, dtype=jnp.int32) % CAP
    owner_index = jnp.arange(ROWS, dtype=jnp.int32) // CAP
    totals = [jax.tree.map(jnp.zeros_like, params) for params in section_params]
    first_out, second_out, first_grad, second_grad = ([], [], [], [])
    for micro_index in range(MB):
        key_live = slot_index < counts[micro_index][owner_index]
        live_rows = key_live.astype(jnp.float32)

        def run_layer(residual, params):
            return layer_apply(params, residual, live_rows, key_live)
        entry_rows = section_input[micro_index].astype(jnp.float32)
        middle_out, back_first = jax.vjp(run_layer, entry_rows, section_params[0])
        middle_low = low(middle_out)
        final_out, back_second = jax.vjp(run_layer, middle_low, section_params[1])
        grad_middle, grads_second = back_second(cotangent[micro_index].astype(jnp.float32))
        grad_entry, grads_first = back_first(low(grad_middle))
        totals[0] = jax.tree.map(jnp.add, totals[0], grads_first)
        totals[1] = jax.tree.map(jnp.add, totals[1], grads_second)
        first_out.append(middle_low)
        second_out.append(final_out)
        first_grad.append(grad_entry)
        second_grad.append(grad_middle)
    acts = jnp.stack([jnp.stack(first_out), jnp.stack(second_out)]).astype(jnp.bfloat16)
    in_grads = jnp.stack([jnp.stack(first_grad), jnp.stack(second_grad)]).astype(jnp.bfloat16)
    stacked = [jnp.stack([totals[0][position], totals[1][position]]) for position in range(8)]
    grad_norm_gain = stacked[0]
    grad_vector_bias = stacked[1]
    grad_qkv = stacked[2]
    grad_head_bias = stacked[3]
    grad_out = stacked[4]
    grad_up = stacked[5]
    grad_up_bias = stacked[6]
    grad_down = stacked[7]
    return (acts, in_grads, grad_norm_gain, grad_vector_bias, grad_qkv, grad_head_bias, grad_out, grad_up, grad_up_bias, grad_down)
```

```python
from functools import partial

import jax
import jax.numpy as jnp
from jax import lax
from jax.experimental import pallas as pl
from jax.experimental.pallas import tpu as pltpu
from jax.sharding import PartitionSpec as P

HD = 64
EPSILON = 1e-06
VMEM_BYTES = 48 * 1024 * 1024


def from_behind(block, axis, distance):
    devices = range(lax.axis_size(axis))
    route = [(i - distance, i) for i in devices if i - distance in devices]
    return lax.ppermute(block, axis, route)


def contract(left, right, left_dim, right_dim):
    return lax.dot_general(
        left,
        right,
        (((left_dim,), (right_dim,)), ((), ())),
        preferred_element_type=jnp.float32,
    )


def product(left, right):
    return contract(left, right, 1, 0)


def product_left(left, right):
    return contract(left, right, 0, 0)


def product_right(left, right):
    return contract(left, right, 1, 1)


def gelu_exact(values):
    return jax.nn.gelu(values, approximate=False)


def normalize(values, gains, shift):
    center = values - jnp.mean(values, axis=-1, keepdims=True)
    inverse = lax.rsqrt(jnp.mean(center * center, axis=-1, keepdims=True) + EPSILON)
    scaled = center * inverse
    return (scaled * gains + shift, scaled, inverse)


def norm_back(grad_normed, scaled, inverse, gains):
    grad_scaled = grad_normed * gains
    return inverse * (
        grad_scaled
        - jnp.mean(grad_scaled, axis=-1, keepdims=True)
        - scaled * jnp.mean(grad_scaled * scaled, axis=-1, keepdims=True)
    )


def attend_kernel(heads, query_ref, held_ref, out_ref, log_ref):
    width = heads * HD
    for head in range(heads):
        keys = held_ref[:, head * HD : (head + 1) * HD]
        values = held_ref[:, width + head * HD : width + (head + 1) * HD]
        queries = query_ref[:, head * HD : (head + 1) * HD]
        scores = product_right(keys, queries) * HD ** (-0.5)
        top = jnp.max(scores, axis=0, keepdims=True)
        weights = jnp.exp(scores - top)
        total = jnp.sum(weights, axis=0, keepdims=True)
        mixed = product_left(values, weights.astype(jnp.bfloat16))
        out_ref[head * HD : (head + 1) * HD, :] = mixed / total
        log_ref[head : head + 1, :] = top + jnp.log(total)


def attend(queries, held, heads):
    rows, width = queries.shape
    length = held.shape[0]
    block = min(rows, 256)
    work = rows * length * width
    return pl.pallas_call(
        partial(attend_kernel, heads),
        grid=(rows // block,),
        in_specs=[
            pl.BlockSpec((block, width), lambda i: (i, 0)),
            pl.BlockSpec((length, 2 * width), lambda i: (0, 0)),
        ],
        out_specs=[
            pl.BlockSpec((width, block), lambda i: (0, i)),
            pl.BlockSpec((heads, block), lambda i: (0, i)),
        ],
        out_shape=[
            jax.ShapeDtypeStruct((width, rows), jnp.float32),
            jax.ShapeDtypeStruct((heads, rows), jnp.float32),
        ],
        compiler_params=pltpu.CompilerParams(vmem_limit_bytes=VMEM_BYTES),
        cost_estimate=pl.CostEstimate(
            flops=4 * work, bytes_accessed=4 * length * width, transcendentals=work // HD
        ),
    )(queries, held)


def attend_back_kernel(
    heads, query_ref, held_ref, grad_ref, log_ref, delta_ref, grad_query_ref, grad_held_ref
):
    width = heads * HD
    block = pl.program_id(0)

    @pl.when(block == 0)
    def _():
        grad_held_ref[...] = jnp.zeros_like(grad_held_ref)

    for head in range(heads):
        low, high = head * HD, (head + 1) * HD
        keys = held_ref[:, low:high]
        values = held_ref[:, width + low : width + high]
        queries = query_ref[:, low:high]
        grads = grad_ref[:, low:high]
        scores = product_right(keys, queries) * HD ** (-0.5)
        weights = jnp.exp(scores - log_ref[head : head + 1, :])
        grad_weights = product_right(values, grads)
        grad_scores = weights * (grad_weights - delta_ref[head : head + 1, :])
        grad_scores = grad_scores.astype(jnp.bfloat16)
        grad_query_ref[low:high, :] = product_left(keys, grad_scores) * HD ** (-0.5)
        grad_held_ref[:, low:high] += product(grad_scores, queries) * HD ** (-0.5)
        grad_held_ref[:, width + low : width + high] += product(
            weights.astype(jnp.bfloat16), grads
        )


def attend_back(queries, held, grad_rows, log_total, row_delta, heads):
    rows, width = queries.shape
    length = held.shape[0]
    block = min(rows, 256)
    work = rows * length * width
    return pl.pallas_call(
        partial(attend_back_kernel, heads),
        grid=(rows // block,),
        in_specs=[
            pl.BlockSpec((block, width), lambda i: (i, 0)),
            pl.BlockSpec((length, 2 * width), lambda i: (0, 0)),
            pl.BlockSpec((block, width), lambda i: (i, 0)),
            pl.BlockSpec((heads, block), lambda i: (0, i)),
            pl.BlockSpec((heads, block), lambda i: (0, i)),
        ],
        out_specs=[
            pl.BlockSpec((width, block), lambda i: (0, i)),
            pl.BlockSpec((length, 2 * width), lambda i: (0, 0)),
        ],
        out_shape=[
            jax.ShapeDtypeStruct((width, rows), jnp.float32),
            jax.ShapeDtypeStruct((length, 2 * width), jnp.float32),
        ],
        compiler_params=pltpu.CompilerParams(vmem_limit_bytes=VMEM_BYTES),
        cost_estimate=pl.CostEstimate(
            flops=10 * work, bytes_accessed=12 * length * width, transcendentals=work // HD
        ),
    )(queries, held, grad_rows, log_total, row_delta)


def local(
    section_input,
    cotangent,
    counts,
    norm_gain,
    vector_bias,
    qkv_weight,
    head_bias,
    out_weight,
    up_weight,
    up_bias,
    down_weight,
):
    ctx_count = lax.axis_size("ctx")
    ctx_index = lax.axis_index("ctx")
    tp_count = lax.axis_size("tp")
    tp_index = lax.axis_index("tp")
    section_index = lax.axis_index("section")
    micro_count, capacity, width = section_input.shape
    share = capacity // 2
    half = share // 2
    head_count = head_bias.shape[2]
    local_width = head_count * HD

    small = (norm_gain, vector_bias, head_bias, up_bias)
    packed = jnp.concatenate([member.reshape(-1) for member in small])
    packed_all = lax.all_gather(packed, "ctx", axis=0, tiled=False)
    opened = []
    start = 0
    for member in small:
        part = packed_all[:, start : start + member.size].reshape((ctx_count,) + member.shape[1:])
        part = jnp.moveaxis(part, 0, -2)
        opened.append(part.reshape(part.shape[:-2] + (part.shape[-2] * part.shape[-1],)))
        start += member.size
    gains = opened[0].astype(jnp.float32)
    shifts = opened[1].astype(jnp.float32)
    bias_heads = opened[2].astype(jnp.float32).reshape(2, local_width)
    expand_bias = opened[3].astype(jnp.float32).reshape(-1)
    proj_weight = lax.all_gather(qkv_weight[0], "ctx", axis=1, tiled=True)
    merge_weight = lax.all_gather(out_weight[0], "ctx", axis=1, tiled=True)
    expand_weight = lax.all_gather(up_weight[0], "ctx", axis=0, tiled=True)
    reduce_weight = lax.all_gather(down_weight[0], "ctx", axis=1, tiled=True)

    surplus = jnp.maximum(counts - share, 0)
    deficit = jnp.maximum(share - counts, 0)
    surplus_start = jnp.cumsum(surplus, axis=1) - surplus
    deficit_start = jnp.cumsum(deficit, axis=1) - deficit
    mine = jnp.arange(ctx_count, dtype=jnp.int32) == ctx_index
    my_count = jnp.sum(jnp.where(mine, counts, 0), axis=1)
    my_surplus = jnp.sum(jnp.where(mine, surplus, 0), axis=1)
    my_start = jnp.sum(jnp.where(mine, surplus_start, 0), axis=1)
    slots = (share - half) + jnp.arange(half, dtype=jnp.int32)
    source = (
        deficit_start[:, :, None]
        + slots[None, None, :]
        - counts[:, :, None]
        - my_start[:, None, None]
    )
    free = slots[None, None, :] >= counts[:, :, None]
    past = jnp.arange(share, dtype=jnp.int32)
    chosen = (
        (source[:, :, :, None] == past)
        & free[:, :, :, None]
        & (past[None, :] < my_surplus[:, None])[:, None, None, :]
    ).astype(jnp.bfloat16)
    own_slot = slots[None, :] < my_count[:, None]
    piece = half // tp_count
    strip = width // tp_count

    def spread(rows, first, last):
        picked = lax.dynamic_slice_in_dim(chosen[first:last], tp_index * piece, piece, 2)
        sent = jnp.einsum(
            "mjrc,mcd->mjrd", picked, rows[first:last, share:], preferred_element_type=jnp.float32
        ).astype(jnp.bfloat16)
        got = lax.psum_scatter(sent, "ctx", scatter_dimension=1, tiled=True)[:, 0]
        got = lax.all_gather(got, "tp", axis=1, tiled=True)
        tail = jnp.where(own_slot[first:last, :, None], rows[first:last, share - half : share], got)
        return jnp.concatenate([rows[first:last, : share - half], tail], axis=1)

    def restore(rows, first, last):
        mine_part = lax.dynamic_slice_in_dim(rows[:, share - half :], tp_index * strip, strip, 2)
        every = lax.all_gather(mine_part, "ctx", axis=1, tiled=False)
        back = jnp.einsum(
            "mjrc,mjrd->mcd", chosen[first:last], every, preferred_element_type=jnp.float32
        ).astype(jnp.bfloat16)
        back = lax.all_gather(back, "tp", axis=2, tiled=True)
        tail = jnp.where(own_slot[first:last, :, None], rows[:, share - half :], 0)
        return jnp.concatenate([rows[:, : share - half], tail, back], axis=1)

    entering = jnp.where(section_index == 0, section_input, cotangent)
    entry_first = spread(entering, 0, 1)
    entry_rest = spread(entering, 1, micro_count)
    entry_rows = [entry_first[0]] + [entry_rest[i] for i in range(micro_count - 1)]

    def tp_total(partial_rows):
        return lax.psum(partial_rows.astype(jnp.bfloat16), "tp").astype(jnp.float32)

    def layer_forward(current):
        residual = current.astype(jnp.float32)
        normed, scaled_one, inverse_one = normalize(residual, gains[0], shifts[0])
        normed_low = normed.astype(jnp.bfloat16)
        held_part = jnp.concatenate(
            [
                product(normed_low, proj_weight[1]),
                product(normed_low, proj_weight[2]) + bias_heads[1],
            ],
            axis=1,
        ).astype(jnp.bfloat16)
        held = lax.all_gather(held_part, "ctx", axis=0, tiled=True)
        queries = (product(normed_low, proj_weight[0]) + bias_heads[0]).astype(jnp.bfloat16)
        exact_out, log_total = attend(queries, held, head_count)
        attended = exact_out.astype(jnp.bfloat16)
        middle = residual + tp_total(product_left(attended, merge_weight)) + shifts[1]
        normed_two, scaled_two, inverse_two = normalize(middle, gains[1], shifts[2])
        normed_two_low = normed_two.astype(jnp.bfloat16)
        expanded = product(normed_two_low, expand_weight) + expand_bias
        activated = gelu_exact(expanded).astype(jnp.bfloat16)
        output_rows = middle + tp_total(product(activated, reduce_weight)) + shifts[3]
        kept = (
            scaled_one,
            inverse_one,
            normed_low,
            queries,
            held,
            log_total,
            exact_out,
            attended,
            scaled_two,
            inverse_two,
            normed_two_low,
            expanded,
            activated,
        )
        return output_rows.astype(jnp.bfloat16), kept

    def layer_backward(grad_low, kept):
        (
            scaled_one,
            inverse_one,
            normed_low,
            queries,
            held,
            log_total,
            exact_out,
            attended,
            scaled_two,
            inverse_two,
            normed_two_low,
            expanded,
            activated,
        ) = kept
        grad_rows = grad_low.astype(jnp.float32)
        grad_active = product_right(grad_low, reduce_weight)
        unused, gelu_back = jax.vjp(gelu_exact, expanded)
        grad_expand = gelu_back(grad_active)[0].astype(jnp.bfloat16)
        grad_normed_two = tp_total(product_right(grad_expand, expand_weight))
        grad_reduce = product_left(activated, grad_low)
        grad_shift_three = jnp.sum(grad_rows, axis=0)
        grad_expand_weight = product_left(normed_two_low, grad_expand)
        grad_expand_bias = jnp.sum(grad_expand, axis=0, dtype=jnp.float32)
        grad_gain_two = jnp.sum(grad_normed_two * scaled_two, axis=0)
        grad_shift_two = jnp.sum(grad_normed_two, axis=0)
        grad_middle = grad_rows + norm_back(grad_normed_two, scaled_two, inverse_two, gains[1])
        middle_low = grad_middle.astype(jnp.bfloat16)
        grad_attended = product_right(middle_low, merge_weight).astype(jnp.bfloat16)
        row_delta = jnp.sum(
            (grad_attended.astype(jnp.float32).T * exact_out).reshape(head_count, HD, share), axis=1
        )
        grad_query, grad_held = attend_back(
            queries, held, grad_attended, log_total, row_delta, head_count
        )
        held_low = lax.psum_scatter(
            grad_held.astype(jnp.bfloat16), "ctx", scatter_dimension=0, tiled=True
        )
        grad_merge = product(attended, middle_low)
        grad_shift_one = jnp.sum(middle_low, axis=0, dtype=jnp.float32)
        query_low = grad_query.astype(jnp.bfloat16)
        keys_low = held_low[:, :local_width]
        values_low = held_low[:, local_width:]
        grad_normed = tp_total(
            contract(query_low, proj_weight[0], 0, 1)
            + product_right(keys_low, proj_weight[1])
            + product_right(values_low, proj_weight[2])
        )
        grad_proj = jnp.stack(
            [
                contract(normed_low, query_low, 0, 1),
                product_left(normed_low, keys_low),
                product_left(normed_low, values_low),
            ]
        )
        grad_heads_bias = jnp.stack(
            [
                jnp.sum(query_low, axis=1, dtype=jnp.float32),
                jnp.sum(values_low, axis=0, dtype=jnp.float32),
            ]
        ).reshape(2, head_count, HD)
        grad_gain_one = jnp.sum(grad_normed * scaled_one, axis=0)
        grad_shift_zero = jnp.sum(grad_normed, axis=0)
        grad_entry = grad_middle + norm_back(grad_normed, scaled_one, inverse_one, gains[0])
        grads = (
            jnp.stack([grad_gain_one, grad_gain_two]),
            jnp.stack([grad_shift_zero, grad_shift_one, grad_shift_two, grad_shift_three]),
            grad_heads_bias,
            grad_expand_bias.reshape(-1, HD),
            grad_proj,
            grad_merge,
            grad_expand_weight,
            grad_reduce,
        )
        return (grad_entry.astype(jnp.bfloat16), grads)

    empty_rows = jnp.zeros((share, width), jnp.bfloat16)
    incoming = empty_rows
    produced = []
    memory = []
    for tick_index in range(micro_count + 1):
        own_rows = entry_rows[tick_index] if tick_index < micro_count else empty_rows
        current = jnp.where(section_index == 0, own_rows, incoming)
        output_low, kept = layer_forward(current)
        produced.append(output_low)
        memory.append(kept)
        if tick_index < micro_count:
            incoming = from_behind(output_low, "section", 1)
    acts = restore(
        jnp.stack(
            [
                jnp.where(section_index == 0, produced[i], produced[i + 1])
                for i in range(micro_count)
            ]
        ),
        0,
        micro_count,
    )[None]
    returning = empty_rows
    totals = None
    returned = []
    for tick_index in range(micro_count + 1):
        own_rows = (
            entry_rows[micro_count - 1 - tick_index] if tick_index < micro_count else empty_rows
        )
        current = jnp.where(section_index == 1, own_rows, returning)
        entry_low, grads = layer_backward(current, memory[micro_count - tick_index])
        totals = grads if totals is None else jax.tree.map(jnp.add, totals, grads)
        returned.append(entry_low)
        if tick_index < micro_count:
            returning = from_behind(entry_low, "section", -1)
    grad_inputs = [
        jnp.where(section_index == 0, returned[micro_count - i], returned[micro_count - 1 - i])
        for i in range(micro_count)
    ]
    in_grads = jnp.concatenate(
        [
            restore(grad_inputs[0][None], 0, 1),
            restore(jnp.stack(grad_inputs[1:]), 1, micro_count),
        ]
    )[None]

    def owned(total, dimension):
        return lax.psum_scatter(
            total.astype(jnp.bfloat16), "ctx", scatter_dimension=dimension, tiled=True
        ).astype(jnp.float32)[None]

    small_totals = []
    for total in totals[:4]:
        split = total.reshape(total.shape[:-1] + (ctx_count, total.shape[-1] // ctx_count))
        small_totals.append(jnp.moveaxis(split, -2, 0).reshape(ctx_count, -1))
    small_owned = lax.psum_scatter(
        jnp.concatenate(small_totals, axis=1).astype(jnp.bfloat16),
        "ctx",
        scatter_dimension=0,
        tiled=True,
    )[0].astype(jnp.float32)
    small_out = []
    start = 0
    for member in small:
        small_out.append(small_owned[start : start + member.size].reshape(member.shape))
        start += member.size
    return (
        acts,
        in_grads,
        small_out[0],
        small_out[1],
        owned(totals[4], 1),
        small_out[2],
        owned(totals[5], 1),
        owned(totals[6], 0),
        small_out[3],
        owned(totals[7], 1),
    )


def solution(mesh):
    in_specs = (
        P(None, "ctx", None),
        P(None, "ctx", None),
        P(),
        P("section", None, "ctx"),
        P("section", None, "ctx"),
        P("section", None, "ctx", "tp"),
        P("section", None, "tp", "ctx"),
        P("section", "tp", "ctx"),
        P("section", "ctx", "tp"),
        P("section", "tp", "ctx"),
        P("section", "tp", "ctx"),
    )
    out_specs = (
        P("section", None, "ctx", None),
        P("section", None, "ctx", None),
        P("section", None, "ctx"),
        P("section", None, "ctx"),
        P("section", None, "ctx", "tp"),
        P("section", None, "tp", "ctx"),
        P("section", "tp", "ctx"),
        P("section", "ctx", "tp"),
        P("section", "tp", "ctx"),
        P("section", "tp", "ctx"),
    )
    return jax.shard_map(local, mesh=mesh, in_specs=in_specs, out_specs=out_specs, check_vma=False)
```

```python
from functools import partial

import jax
import jax.numpy as jnp
from jax import lax
from jax.experimental import pallas as pl
from jax.experimental.pallas import tpu as pltpu
from jax.sharding import PartitionSpec as P

HD = 64
EPSILON = 1e-06
VMEM_BYTES = 48 * 1024 * 1024


def from_behind(block, axis, distance):
    devices = range(lax.axis_size(axis))
    route = [(i - distance, i) for i in devices if i - distance in devices]
    return lax.ppermute(block, axis, route)


def contract(left, right, left_dim, right_dim):
    return lax.dot_general(
        left,
        right,
        (((left_dim,), (right_dim,)), ((), ())),
        preferred_element_type=jnp.float32,
    )


def product(left, right):
    return contract(left, right, 1, 0)


def product_left(left, right):
    return contract(left, right, 0, 0)


def product_right(left, right):
    return contract(left, right, 1, 1)


def gelu_exact(values):
    return jax.nn.gelu(values, approximate=False)


def normalize(values, gains, shift):
    center = values - jnp.mean(values, axis=-1, keepdims=True)
    inverse = lax.rsqrt(jnp.mean(center * center, axis=-1, keepdims=True) + EPSILON)
    scaled = center * inverse
    return (scaled * gains + shift, scaled, inverse)


def norm_back(grad_normed, scaled, inverse, gains):
    grad_scaled = grad_normed * gains
    return inverse * (
        grad_scaled
        - jnp.mean(grad_scaled, axis=-1, keepdims=True)
        - scaled * jnp.mean(grad_scaled * scaled, axis=-1, keepdims=True)
    )


def attend_kernel(heads, query_ref, held_ref, out_ref, log_ref):
    width = heads * HD
    for head in range(heads):
        keys = held_ref[:, head * HD : (head + 1) * HD]
        values = held_ref[:, width + head * HD : width + (head + 1) * HD]
        queries = query_ref[:, head * HD : (head + 1) * HD]
        scores = product_right(keys, queries) * HD ** (-0.5)
        top = jnp.max(scores, axis=0, keepdims=True)
        weights = jnp.exp(scores - top)
        total = jnp.sum(weights, axis=0, keepdims=True)
        mixed = product_left(values, weights.astype(jnp.bfloat16))
        out_ref[head * HD : (head + 1) * HD, :] = mixed / total
        log_ref[head : head + 1, :] = top + jnp.log(total)


def attend(queries, held, heads):
    rows, width = queries.shape
    length = held.shape[0]
    block = min(rows, 256)
    work = rows * length * width
    return pl.pallas_call(
        partial(attend_kernel, heads),
        grid=(rows // block,),
        in_specs=[
            pl.BlockSpec((block, width), lambda i: (i, 0)),
            pl.BlockSpec((length, 2 * width), lambda i: (0, 0)),
        ],
        out_specs=[
            pl.BlockSpec((width, block), lambda i: (0, i)),
            pl.BlockSpec((heads, block), lambda i: (0, i)),
        ],
        out_shape=[
            jax.ShapeDtypeStruct((width, rows), jnp.float32),
            jax.ShapeDtypeStruct((heads, rows), jnp.float32),
        ],
        compiler_params=pltpu.CompilerParams(vmem_limit_bytes=VMEM_BYTES),
        cost_estimate=pl.CostEstimate(
            flops=4 * work, bytes_accessed=4 * length * width, transcendentals=work // HD
        ),
    )(queries, held)


def attend_back_kernel(
    heads, query_ref, held_ref, grad_ref, log_ref, delta_ref, grad_query_ref, grad_held_ref
):
    width = heads * HD
    block = pl.program_id(0)

    @pl.when(block == 0)
    def _():
        grad_held_ref[...] = jnp.zeros_like(grad_held_ref)

    for head in range(heads):
        low, high = head * HD, (head + 1) * HD
        keys = held_ref[:, low:high]
        values = held_ref[:, width + low : width + high]
        queries = query_ref[:, low:high]
        grads = grad_ref[:, low:high]
        scores = product_right(keys, queries) * HD ** (-0.5)
        weights = jnp.exp(scores - log_ref[head : head + 1, :])
        grad_weights = product_right(values, grads)
        grad_scores = weights * (grad_weights - delta_ref[head : head + 1, :])
        grad_scores = grad_scores.astype(jnp.bfloat16)
        grad_query_ref[low:high, :] = product_left(keys, grad_scores) * HD ** (-0.5)
        grad_held_ref[:, low:high] += product(grad_scores, queries) * HD ** (-0.5)
        grad_held_ref[:, width + low : width + high] += product(
            weights.astype(jnp.bfloat16), grads
        )


def attend_back(queries, held, grad_rows, log_total, row_delta, heads):
    rows, width = queries.shape
    length = held.shape[0]
    block = min(rows, 256)
    work = rows * length * width
    return pl.pallas_call(
        partial(attend_back_kernel, heads),
        grid=(rows // block,),
        in_specs=[
            pl.BlockSpec((block, width), lambda i: (i, 0)),
            pl.BlockSpec((length, 2 * width), lambda i: (0, 0)),
            pl.BlockSpec((block, width), lambda i: (i, 0)),
            pl.BlockSpec((heads, block), lambda i: (0, i)),
            pl.BlockSpec((heads, block), lambda i: (0, i)),
        ],
        out_specs=[
            pl.BlockSpec((width, block), lambda i: (0, i)),
            pl.BlockSpec((length, 2 * width), lambda i: (0, 0)),
        ],
        out_shape=[
            jax.ShapeDtypeStruct((width, rows), jnp.float32),
            jax.ShapeDtypeStruct((length, 2 * width), jnp.float32),
        ],
        compiler_params=pltpu.CompilerParams(vmem_limit_bytes=VMEM_BYTES),
        cost_estimate=pl.CostEstimate(
            flops=10 * work, bytes_accessed=12 * length * width, transcendentals=work // HD
        ),
    )(queries, held, grad_rows, log_total, row_delta)


def local(
    section_input,
    cotangent,
    counts,
    norm_gain,
    vector_bias,
    qkv_weight,
    head_bias,
    out_weight,
    up_weight,
    up_bias,
    down_weight,
):
    ctx_count = lax.axis_size("ctx")
    ctx_index = lax.axis_index("ctx")
    tp_count = lax.axis_size("tp")
    tp_index = lax.axis_index("tp")
    section_index = lax.axis_index("section")
    micro_count, capacity, width = section_input.shape
    share = capacity // 2
    half = share // 2
    head_count = head_bias.shape[2]
    local_width = head_count * HD

    small = (norm_gain, vector_bias, head_bias, up_bias)
    packed = jnp.concatenate([member.reshape(-1) for member in small])
    packed_all = lax.all_gather(packed, "ctx", axis=0, tiled=False)
    opened = []
    start = 0
    for member in small:
        part = packed_all[:, start : start + member.size].reshape((ctx_count,) + member.shape[1:])
        part = jnp.moveaxis(part, 0, -2)
        opened.append(part.reshape(part.shape[:-2] + (part.shape[-2] * part.shape[-1],)))
        start += member.size
    gains = opened[0].astype(jnp.float32)
    shifts = opened[1].astype(jnp.float32)
    bias_heads = opened[2].astype(jnp.float32).reshape(2, local_width)
    expand_bias = opened[3].astype(jnp.float32).reshape(-1)
    proj_weight = lax.all_gather(qkv_weight[0], "ctx", axis=1, tiled=True)
    merge_weight = lax.all_gather(out_weight[0], "ctx", axis=1, tiled=True)
    expand_weight = lax.all_gather(up_weight[0], "ctx", axis=0, tiled=True)
    reduce_weight = lax.all_gather(down_weight[0], "ctx", axis=1, tiled=True)

    surplus = jnp.maximum(counts - share, 0)
    deficit = jnp.maximum(share - counts, 0)
    surplus_start = jnp.cumsum(surplus, axis=1) - surplus
    deficit_start = jnp.cumsum(deficit, axis=1) - deficit
    mine = jnp.arange(ctx_count, dtype=jnp.int32) == ctx_index
    my_count = jnp.sum(jnp.where(mine, counts, 0), axis=1)
    my_surplus = jnp.sum(jnp.where(mine, surplus, 0), axis=1)
    my_start = jnp.sum(jnp.where(mine, surplus_start, 0), axis=1)
    slots = (share - half) + jnp.arange(half, dtype=jnp.int32)
    source = (
        deficit_start[:, :, None]
        + slots[None, None, :]
        - counts[:, :, None]
        - my_start[:, None, None]
    )
    free = slots[None, None, :] >= counts[:, :, None]
    past = jnp.arange(share, dtype=jnp.int32)
    chosen = (
        (source[:, :, :, None] == past)
        & free[:, :, :, None]
        & (past[None, :] < my_surplus[:, None])[:, None, None, :]
    ).astype(jnp.bfloat16)
    own_slot = slots[None, :] < my_count[:, None]
    piece = half // tp_count
    strip = width // tp_count

    def spread(rows, first, last):
        picked = lax.dynamic_slice_in_dim(chosen[first:last], tp_index * piece, piece, 2)
        sent = jnp.einsum(
            "mjrc,mcd->mjrd", picked, rows[first:last, share:], preferred_element_type=jnp.float32
        ).astype(jnp.bfloat16)
        got = lax.psum_scatter(sent, "ctx", scatter_dimension=1, tiled=True)[:, 0]
        got = lax.all_gather(got, "tp", axis=1, tiled=True)
        tail = jnp.where(own_slot[first:last, :, None], rows[first:last, share - half : share], got)
        return jnp.concatenate([rows[first:last, : share - half], tail], axis=1)

    def restore(rows, first, last):
        mine_part = lax.dynamic_slice_in_dim(rows[:, share - half :], tp_index * strip, strip, 2)
        every = lax.all_gather(mine_part, "ctx", axis=1, tiled=False)
        back = jnp.einsum(
            "mjrc,mjrd->mcd", chosen[first:last], every, preferred_element_type=jnp.float32
        ).astype(jnp.bfloat16)
        back = lax.all_gather(back, "tp", axis=2, tiled=True)
        tail = jnp.where(own_slot[first:last, :, None], rows[:, share - half :], 0)
        return jnp.concatenate([rows[:, : share - half], tail, back], axis=1)

    entering = jnp.where(section_index == 0, section_input, cotangent)
    entry_first = spread(entering, 0, 1)
    entry_rest = spread(entering, 1, micro_count)
    entry_rows = [entry_first[0]] + [entry_rest[i] for i in range(micro_count - 1)]

    def swap(rows, distance):
        return lax.ppermute(rows, "tp", [(i, i ^ distance) for i in range(tp_count)])

    def joined(rows):
        other = swap(rows, 1)
        even = tp_index % 2 == 0
        return jnp.concatenate([jnp.where(even, rows, other), jnp.where(even, other, rows)], axis=0)

    def pair_half(rows, place):
        return jnp.where(place == 0, rows[:half], rows[half:])

    def tp_total(partial_rows):
        rows = partial_rows.astype(jnp.bfloat16)
        place = tp_index % 2
        total = pair_half(rows, place).astype(jnp.float32)
        total = total + swap(pair_half(rows, 1 - place), 1).astype(jnp.float32)
        distance = 2
        while distance < tp_count:
            low = total.astype(jnp.bfloat16)
            total = low.astype(jnp.float32) + swap(low, distance).astype(jnp.float32)
            distance *= 2
        return joined(total.astype(jnp.bfloat16)).astype(jnp.float32)

    def to_section(rows, distance):
        return joined(from_behind(pair_half(rows, tp_index % 2), "section", distance))

    def layer_forward(current):
        residual = current.astype(jnp.float32)
        normed, scaled_one, inverse_one = normalize(residual, gains[0], shifts[0])
        normed_low = normed.astype(jnp.bfloat16)
        held_part = jnp.concatenate(
            [
                product(normed_low, proj_weight[1]),
                product(normed_low, proj_weight[2]) + bias_heads[1],
            ],
            axis=1,
        ).astype(jnp.bfloat16)
        held = lax.all_gather(held_part, "ctx", axis=0, tiled=True)
        queries = (product(normed_low, proj_weight[0]) + bias_heads[0]).astype(jnp.bfloat16)
        exact_out, log_total = attend(queries, held, head_count)
        attended = exact_out.astype(jnp.bfloat16)
        middle = residual + tp_total(product_left(attended, merge_weight)) + shifts[1]
        normed_two, scaled_two, inverse_two = normalize(middle, gains[1], shifts[2])
        normed_two_low = normed_two.astype(jnp.bfloat16)
        expanded = product(normed_two_low, expand_weight) + expand_bias
        activated = gelu_exact(expanded).astype(jnp.bfloat16)
        output_rows = middle + tp_total(product(activated, reduce_weight)) + shifts[3]
        kept = (
            scaled_one,
            inverse_one,
            normed_low,
            queries,
            held,
            log_total,
            exact_out,
            attended,
            scaled_two,
            inverse_two,
            normed_two_low,
            expanded,
            activated,
        )
        return output_rows.astype(jnp.bfloat16), kept

    def layer_backward(grad_low, kept):
        (
            scaled_one,
            inverse_one,
            normed_low,
            queries,
            held,
            log_total,
            exact_out,
            attended,
            scaled_two,
            inverse_two,
            normed_two_low,
            expanded,
            activated,
        ) = kept
        grad_rows = grad_low.astype(jnp.float32)
        grad_active = product_right(grad_low, reduce_weight)
        unused, gelu_back = jax.vjp(gelu_exact, expanded)
        grad_expand = gelu_back(grad_active)[0].astype(jnp.bfloat16)
        grad_normed_two = tp_total(product_right(grad_expand, expand_weight))
        grad_reduce = product_left(activated, grad_low)
        grad_shift_three = jnp.sum(grad_rows, axis=0)
        grad_expand_weight = product_left(normed_two_low, grad_expand)
        grad_expand_bias = jnp.sum(grad_expand, axis=0, dtype=jnp.float32)
        grad_gain_two = jnp.sum(grad_normed_two * scaled_two, axis=0)
        grad_shift_two = jnp.sum(grad_normed_two, axis=0)
        grad_middle = grad_rows + norm_back(grad_normed_two, scaled_two, inverse_two, gains[1])
        middle_low = grad_middle.astype(jnp.bfloat16)
        grad_attended = product_right(middle_low, merge_weight).astype(jnp.bfloat16)
        row_delta = jnp.sum(
            (grad_attended.astype(jnp.float32).T * exact_out).reshape(head_count, HD, share), axis=1
        )
        grad_query, grad_held = attend_back(
            queries, held, grad_attended, log_total, row_delta, head_count
        )
        held_low = lax.psum_scatter(
            grad_held.astype(jnp.bfloat16), "ctx", scatter_dimension=0, tiled=True
        )
        grad_merge = product(attended, middle_low)
        grad_shift_one = jnp.sum(middle_low, axis=0, dtype=jnp.float32)
        query_low = grad_query.astype(jnp.bfloat16)
        keys_low = held_low[:, :local_width]
        values_low = held_low[:, local_width:]
        grad_normed = tp_total(
            contract(query_low, proj_weight[0], 0, 1)
            + product_right(keys_low, proj_weight[1])
            + product_right(values_low, proj_weight[2])
        )
        grad_proj = jnp.stack(
            [
                contract(normed_low, query_low, 0, 1),
                product_left(normed_low, keys_low),
                product_left(normed_low, values_low),
            ]
        )
        grad_heads_bias = jnp.stack(
            [
                jnp.sum(query_low, axis=1, dtype=jnp.float32),
                jnp.sum(values_low, axis=0, dtype=jnp.float32),
            ]
        ).reshape(2, head_count, HD)
        grad_gain_one = jnp.sum(grad_normed * scaled_one, axis=0)
        grad_shift_zero = jnp.sum(grad_normed, axis=0)
        grad_entry = grad_middle + norm_back(grad_normed, scaled_one, inverse_one, gains[0])
        grads = (
            jnp.stack([grad_gain_one, grad_gain_two]),
            jnp.stack([grad_shift_zero, grad_shift_one, grad_shift_two, grad_shift_three]),
            grad_heads_bias,
            grad_expand_bias.reshape(-1, HD),
            grad_proj,
            grad_merge,
            grad_expand_weight,
            grad_reduce,
        )
        return (grad_entry.astype(jnp.bfloat16), grads)

    empty_rows = jnp.zeros((share, width), jnp.bfloat16)
    incoming = empty_rows
    produced = []
    memory = []
    for tick_index in range(micro_count + 1):
        own_rows = entry_rows[tick_index] if tick_index < micro_count else empty_rows
        current = jnp.where(section_index == 0, own_rows, incoming)
        output_low, kept = layer_forward(current)
        produced.append(output_low)
        memory.append(kept)
        if tick_index < micro_count:
            incoming = to_section(output_low, 1)
    acts = restore(
        jnp.stack(
            [
                jnp.where(section_index == 0, produced[i], produced[i + 1])
                for i in range(micro_count)
            ]
        ),
        0,
        micro_count,
    )[None]
    returning = empty_rows
    totals = None
    returned = []
    for tick_index in range(micro_count + 1):
        own_rows = (
            entry_rows[micro_count - 1 - tick_index] if tick_index < micro_count else empty_rows
        )
        current = jnp.where(section_index == 1, own_rows, returning)
        entry_low, grads = layer_backward(current, memory[micro_count - tick_index])
        totals = grads if totals is None else jax.tree.map(jnp.add, totals, grads)
        returned.append(entry_low)
        if tick_index < micro_count:
            returning = to_section(entry_low, -1)
    grad_inputs = [
        jnp.where(section_index == 0, returned[micro_count - i], returned[micro_count - 1 - i])
        for i in range(micro_count)
    ]
    in_grads = jnp.concatenate(
        [
            restore(grad_inputs[0][None], 0, 1),
            restore(jnp.stack(grad_inputs[1:]), 1, micro_count),
        ]
    )[None]

    def owned(total, dimension):
        return lax.psum_scatter(
            total.astype(jnp.bfloat16), "ctx", scatter_dimension=dimension, tiled=True
        ).astype(jnp.float32)[None]

    small_totals = []
    for total in totals[:4]:
        split = total.reshape(total.shape[:-1] + (ctx_count, total.shape[-1] // ctx_count))
        small_totals.append(jnp.moveaxis(split, -2, 0).reshape(ctx_count, -1))
    small_owned = lax.psum_scatter(
        jnp.concatenate(small_totals, axis=1).astype(jnp.bfloat16),
        "ctx",
        scatter_dimension=0,
        tiled=True,
    )[0].astype(jnp.float32)
    small_out = []
    start = 0
    for member in small:
        small_out.append(small_owned[start : start + member.size].reshape(member.shape))
        start += member.size
    return (
        acts,
        in_grads,
        small_out[0],
        small_out[1],
        owned(totals[4], 1),
        small_out[2],
        owned(totals[5], 1),
        owned(totals[6], 0),
        small_out[3],
        owned(totals[7], 1),
    )


def solution(mesh):
    in_specs = (
        P(None, "ctx", None),
        P(None, "ctx", None),
        P(),
        P("section", None, "ctx"),
        P("section", None, "ctx"),
        P("section", None, "ctx", "tp"),
        P("section", None, "tp", "ctx"),
        P("section", "tp", "ctx"),
        P("section", "ctx", "tp"),
        P("section", "tp", "ctx"),
        P("section", "tp", "ctx"),
    )
    out_specs = (
        P("section", None, "ctx", None),
        P("section", None, "ctx", None),
        P("section", None, "ctx"),
        P("section", None, "ctx"),
        P("section", None, "ctx", "tp"),
        P("section", None, "tp", "ctx"),
        P("section", "tp", "ctx"),
        P("section", "ctx", "tp"),
        P("section", "tp", "ctx"),
        P("section", "tp", "ctx"),
    )
    return jax.shard_map(local, mesh=mesh, in_specs=in_specs, out_specs=out_specs, check_vma=False)
```
